32 devices in a mesh: state: 2 (over y), mode: 16 (over z, x, core).
Axes of the slice: x: 2, y: 2, z: 4, core: 2. Of those that a mesh axis runs over, the one named last changes fastest.
Arguments:
- coeffs: float32 [2, 128, 4096], P('state', 'mode'), may hold values from -0.375 to 0.375
- diag_h2: float32 [2, 32, 4096], P('state'), may hold values from -0.75 to 0.75
- diag_h3: float32 [2, 32, 4096], P('state'), may hold values from -0.75 to 0.75
- diag_v1: float32 [2, 32, 128], P('state', None, 'mode'), may hold values from -1.5 to 1.5
- coup_h2: float32 [32, 4096], replicated, may hold values from -0.75 to 0.75
- coup_h3: float32 [32, 4096], replicated, may hold values from -0.75 to 0.75
- coup_v1: float32 [32, 128], P(None, 'mode'), may hold values from -1.5 to 1.5
- pairs: int32 [32, 3], replicated, may hold values from 0 to 31, as said below
Outputs:
- action: float32 [2, 128, 4096], P('state', 'mode')
- diag_field: float32 [2, 64, 2048], P('state', 'mode')
- pair_field: float32 [2, 64, 1984], P('state', 'mode')
The draws below stay inside these ranges and needn't reach their ends.
Inputs may be any that keep to these rules, and one draw needn't show every extreme that they name: `pairs`: each row is (target state, source state, coupling term); the source differs from the target; every state is the target of at most 31 rows, and one state of exactly 31.
All inputs are finite; a program needn't handle non-finite values.
Results may differ from the reference program's by a relative error of at most 0.0001.
Values sent between devices are 32-bit elements; how exact they have to be, the bound alone decides.
A program may use at most 64 MiB of HBM per device.

```python
import jax
import jax.numpy as jnp
from jax import lax

N2 = 64
N3 = 64
NDIAG = 32
NCOUP = 32
STATES = 2
G1 = 128
NPAIRS = 32
MAXP = 31


def draw_pairs(key, part):
    subkeys = jax.random.split(key, 5)
    order_states = jax.random.permutation(subkeys[0], STATES).astype(jnp.int32)
    remaining = NPAIRS - MAXP
    half_count = remaining // 2
    crowded = jnp.full((MAXP,), order_states[0], jnp.int32)
    spread = order_states[1 + jnp.arange(half_count, dtype=jnp.int32) % (STATES - 1)]
    random_part = order_states[1 + jax.random.randint(subkeys[1], (remaining - half_count,), 0, STATES - 1)]
    targets = jnp.concatenate([crowded, spread, random_part]).astype(jnp.int32)
    targets = targets[jax.random.permutation(subkeys[2], NPAIRS)]
    sources = (targets + jax.random.randint(subkeys[3], (NPAIRS,), 1, STATES)) % STATES
    term_ids = jax.random.randint(subkeys[4], (NPAIRS,), 0, NCOUP)
    return jnp.stack([targets, sources.astype(jnp.int32), term_ids.astype(jnp.int32)], axis=1).astype(jnp.int32)


def block_scale(key, dims, cuts, least, top_value):
    level, own = 1.0, jax.random.fold_in(key, 6)
    for dim, blocks in cuts:
        heights = jnp.exp(jax.random.uniform(jax.random.fold_in(own, dim), (blocks,), jnp.float32, least / len(cuts), top_value / len(cuts)))
        level = level * jnp.repeat(heights, dims[dim] // blocks).reshape([-1 if axis == dim else 1 for axis in range(len(dims))])
    return level


def normal_values(own_key, extent, scale, most, pieces=(), kind=jnp.bfloat16):
    drawn = jax.random.normal(own_key, extent, jnp.float32) * scale
    if len(pieces) > 0:
        drawn = block_scale(own_key, extent, pieces, -0.22, 0.18) * drawn
    return jnp.clip(drawn, min=-most, max=most).astype(kind)


def setup_inputs(seed: int = 0) -> dict:
    keys = jax.random.split(jax.random.key(seed), 9)
    coeffs = normal_values(keys[0], (STATES, G1, N2 * N3), (4 * N3) ** -0.5, 0.375, ((0, 2), (1, 16)), jnp.float32)
    diag_h2 = normal_values(keys[1], (STATES, NDIAG, N2 * N2), N2 ** -0.5, 0.75, ((0, 2),), jnp.float32)
    diag_h3 = normal_values(keys[2], (STATES, NDIAG, N3 * N3), N3 ** -0.5, 0.75, ((0, 2),), jnp.float32)
    diag_v1 = jnp.clip(jax.random.uniform(keys[3], (STATES, NDIAG, G1), jnp.float32, -1.5, 1.5) * block_scale(keys[3], (STATES, NDIAG, G1), ((0, 2), (2, 16)), -0.4, 0.0), -1.5, 1.5)
    coup_h2 = normal_values(keys[4], (NCOUP, N2 * N2), N2 ** -0.5, 0.75, (), jnp.float32)
    coup_h3 = normal_values(keys[5], (NCOUP, N3 * N3), N3 ** -0.5, 0.75, (), jnp.float32)
    coup_v1 = jnp.clip(jax.random.uniform(keys[6], (NCOUP, G1), jnp.float32, -1.5, 1.5) * block_scale(keys[6], (NCOUP, G1), ((1, 16),), -0.4, 0.0), -1.5, 1.5)
    pairs = draw_pairs(jax.random.fold_in(keys[8], 71), 0)
    return {"coeffs": coeffs, "diag_h2": diag_h2, "diag_h3": diag_h3, "diag_v1": diag_v1, "coup_h2": coup_h2, "coup_h3": coup_h3, "coup_v1": coup_v1, "pairs": pairs}


HIGH = lax.Precision.HIGHEST


def reference(coeffs, diag_h2, diag_h3, diag_v1, coup_h2, coup_h3, coup_v1, pairs):
    tensors = coeffs.reshape(STATES, G1, N2, N3)
    diag_h2 = diag_h2.reshape(STATES, NDIAG, N2, N2)
    diag_h3 = diag_h3.reshape(STATES, NDIAG, N3, N3)
    coup_h2 = coup_h2.reshape(NCOUP, N2, N2)
    coup_h3 = coup_h3.reshape(NCOUP, N3, N3)
    actions = []
    diag_list = []
    for state_index in range(STATES):
        tensor = tensors[state_index]

        def diag_term(accumulated, inputs, tensor=tensor):
            left_op, right_op, weights = inputs
            product = jnp.einsum('gac,dc->gad', tensor, right_op, precision=HIGH)
            action = jnp.einsum('ea,gad->ged', left_op, product, precision=HIGH) * weights[:, None, None]
            weighted = tensor * weights[:, None, None]
            field_block = jnp.einsum('gac,gbc->ab', weighted, product, precision=HIGH)
            return accumulated + action, field_block

        accumulated, fields = lax.scan(diag_term, jnp.zeros((G1, N2, N3), jnp.float32),
                                       (diag_h2[state_index], diag_h3[state_index], diag_v1[state_index]))
        actions.append(accumulated)
        diag_list.append(fields)
    action_all = jnp.stack(actions)
    diag_fields = jnp.stack(diag_list)
    targets = pairs[:, 0]
    positions = jnp.arange(NPAIRS, dtype=jnp.int32)
    earlier_same = (targets[:, None] == targets[None, :]) & (positions[None, :] < positions[:, None])
    slot_ranks = jnp.sum(earlier_same.astype(jnp.int32), axis=1).astype(jnp.int32)

    def pair_term(carried, inputs):
        action_sum, pair_fields = carried
        target_id, source_id, term_id, slot_rank = inputs
        product = jnp.einsum('gac,dc->gad', tensors[source_id], coup_h3[term_id], precision=HIGH)
        weights = coup_v1[term_id]
        action = jnp.einsum('ea,gad->ged', coup_h2[term_id], product, precision=HIGH) * weights[:, None, None]
        weighted = tensors[target_id] * weights[:, None, None]
        field_block = jnp.einsum('gac,gbc->ab', weighted, product, precision=HIGH)
        action_sum = action_sum.at[target_id].add(action)
        pair_fields = pair_fields.at[target_id, slot_rank].set(field_block)
        return (action_sum, pair_fields), None

    start_fields = jnp.zeros((STATES, MAXP, N2, N2), jnp.float32)
    (action_all, pair_fields), _ = lax.scan(pair_term, (action_all, start_fields),
                                            (pairs[:, 0], pairs[:, 1], pairs[:, 2], slot_ranks))
    action = action_all.reshape(STATES, G1, N2 * N3)
    diag_field = diag_fields.transpose(0, 2, 1, 3).reshape(STATES, N2, NDIAG * N2)
    pair_field = pair_fields.transpose(0, 2, 1, 3).reshape(STATES, N2, MAXP * N2)
    return (action, diag_field, pair_field)
```

```python
import jax
import jax.numpy as jnp
from jax import lax
from jax.sharding import PartitionSpec as P

N2 = 64
N3 = 64
PAIRS_MEAN = 16


HIGH = lax.Precision.HIGH


def reduce_rows(partials):
    both = jnp.concatenate(partials, axis=1)
    rows = lax.psum_scatter(both, "mode", scatter_dimension=0, tiled=True)
    return rows[:, : partials[0].shape[1]], rows[:, partials[0].shape[1] :]


def pair_block(gathered, coup_h2, coup_h3, coup_v1, chosen, is_valid):
    target_ids = chosen[:, 0]
    source_ids = chosen[:, 1]
    term_ids = chosen[:, 2]
    product = jnp.einsum("pgac,pdc->pgad", gathered[source_ids], coup_h3[term_ids], precision=HIGH)
    weights = coup_v1[term_ids] * is_valid[:, None]
    action = (
        jnp.einsum("pea,pgad->pged", coup_h2[term_ids], product, precision=HIGH)
        * weights[:, :, None, None]
    )
    weighted = gathered[target_ids] * weights[:, :, None, None]
    fields = jnp.einsum("pgac,pgbc->pab", weighted, product, precision=HIGH)
    return (action, fields)


def per_device(coeffs, diag_h2, diag_h3, diag_v1, coup_h2, coup_h3, coup_v1, pairs):
    rows_here = coeffs.shape[1]
    width2 = N2
    width3 = N3
    own_terms = diag_h2.shape[1]
    left_ops = diag_h2[0].reshape(own_terms, width2, width2)
    right_ops = diag_h3[0].reshape(own_terms, width3, width3)
    coup_left = coup_h2.reshape(coup_h2.shape[0], width2, width2)
    coup_right = coup_h3.reshape(coup_h3.shape[0], width3, width3)
    states = lax.axis_size("state")
    npairs = pairs.shape[0]
    most_slots = min(3 * PAIRS_MEAN, states * PAIRS_MEAN - 1)
    myself = lax.axis_index("state")
    tensor = coeffs[0].reshape(rows_here, width2, width3)
    gathered = lax.all_gather(coeffs, "state", axis=0, tiled=True).reshape(
        states, rows_here, width2, width3
    )
    diag_product = jnp.einsum("gac,tdc->tgad", tensor, right_ops, precision=HIGH)
    diag_terms = jnp.einsum("tea,tgad->tged", left_ops, diag_product, precision=HIGH)
    diag_action = jnp.sum(diag_terms * diag_v1[0][:, :, None, None], axis=0)
    diag_weighted = tensor[None] * diag_v1[0][:, :, None, None]
    diag_fields = jnp.einsum("tgac,tgbc->atb", diag_weighted, diag_product, precision=HIGH)
    diag_fields = diag_fields.reshape(width2, own_terms * width2)
    is_mine = pairs[:, 0] == myself
    slot_rank = jnp.cumsum(is_mine.astype(jnp.int32)) - 1
    owned_ids = jnp.arange(PAIRS_MEAN, dtype=jnp.int32) * states + myself
    chosen = pairs[owned_ids]
    is_valid = jnp.ones((PAIRS_MEAN,), jnp.float32)
    state_ids = jnp.arange(states, dtype=jnp.int32)

    def run_block(block_index, carried):
        pair_sum, fields = carried
        first_slot = block_index * 8
        part_chosen = lax.dynamic_slice_in_dim(chosen, first_slot, 8, 0)
        part_valid = lax.dynamic_slice_in_dim(is_valid, first_slot, 8, 0)
        action, block_fields = pair_block(
            gathered, coup_left, coup_right, coup_v1, part_chosen, part_valid
        )
        onehot = (part_chosen[:, 0][:, None] == state_ids[None, :]).astype(jnp.float32)
        pair_sum = pair_sum + jnp.einsum("ps,pged->sged", onehot, action, precision=HIGH)
        fields = lax.dynamic_update_slice_in_dim(fields, block_fields, first_slot, 0)
        return (pair_sum, fields)

    start_sum = jnp.zeros((states, rows_here, width2, width3), jnp.float32)
    start_fields = jnp.zeros((PAIRS_MEAN, width2, width2), jnp.float32)
    pair_sum, fields = lax.fori_loop(0, PAIRS_MEAN // 8, run_block, (start_sum, start_fields))
    received = lax.psum_scatter(
        pair_sum.reshape(states, rows_here, width2 * width3),
        "state",
        scatter_dimension=0,
        tiled=True,
    )
    accumulated = diag_action + received[0].reshape(rows_here, width2, width3)
    spread_fields = fields.transpose(1, 0, 2).reshape(width2, PAIRS_MEAN * width2)
    diag_rows, spread_rows = reduce_rows((diag_fields, spread_fields))
    share_rows = spread_rows.shape[0]
    collected = lax.all_gather(spread_rows[None], "state", axis=0, tiled=True)
    stacked = collected.reshape(states, share_rows, PAIRS_MEAN, width2).transpose(2, 0, 1, 3)
    stacked = stacked.reshape(npairs, share_rows * width2)
    picked_mask = (
        (slot_rank[None, :] == jnp.arange(most_slots, dtype=jnp.int32)[:, None]) & is_mine[None, :]
    ).astype(jnp.float32)
    picked = jnp.dot(picked_mask, stacked, precision=lax.Precision.HIGHEST)
    pair_rows = picked.reshape(most_slots, share_rows, width2).transpose(1, 0, 2)
    pair_rows = pair_rows.reshape(share_rows, most_slots * width2)
    action_out = accumulated.reshape(1, rows_here, width2 * width3)
    return (action_out, diag_rows[None], pair_rows[None])


def solution(mesh):
    placed = (
        P("state", "mode", None),
        P("state", None, None),
        P("state", None, None),
        P("state", None, "mode"),
        P(),
        P(),
        P(None, "mode"),
        P(),
    )
    return jax.shard_map(
        per_device,
        mesh=mesh,
        in_specs=placed,
        out_specs=(P("state", "mode", None), P("state", "mode", None), P("state", "mode", None)),
        check_vma=False,
    )
```

```python
import functools

import jax
import jax.numpy as jnp
from jax import lax
from jax.experimental import pallas as pl
from jax.experimental.pallas import tpu as pltpu
from jax.sharding import PartitionSpec as P

MESH = pl.DeviceIdType.MESH
F32 = jnp.float32
BF16 = jnp.bfloat16


def split(value):
    high = value.astype(BF16)
    return high, (value - high.astype(F32)).astype(BF16)


def dot_rows(left, right):
    return lax.dot_general(left, right, (((1,), (1,)), ((), ())), preferred_element_type=F32)


def dot(left, right):
    return jnp.dot(left, right, preferred_element_type=F32)


def flag(condition):
    return jnp.where(condition, 1.0, 0.0).astype(F32)


def kernel(
    a_ref, dh2, dh3, ch2, ch3, dv1, cv1, pairs, slots,
    action_ref, diag_ref, pair_ref,
    gath, a3, aa, hh, hp, xh, xl, yh, yl, psum, arecv, gfield, rows3,
    buf0, buf1, buf2, ra0, ra1, ra2, sb0, sb1, sb2, rb0, rb1, rb2, sc0, sc1, sc2, rc0, rc1, rc2,
    send, recv, *, modes
):
    states, grid = gath.shape[0], gath.shape[1]
    n = a_ref.shape[-1]
    half = n // 2
    count = dh2.shape[0] // 2
    pcount = yh.shape[0] // n
    ring = modes // 4
    share = n // modes
    bufs, ras, sbs = (buf0, buf1, buf2), (ra0, ra1, ra2), (sb0, sb1, sb2)
    rbs, scs, rcs = (rb0, rb1, rb2), (sc0, sc1, sc2), (rc0, rc1, rc2)

    st = lax.axis_index("state")
    md = lax.axis_index("mode")
    core = lax.rem(md, 2)
    x = lax.rem(lax.div(md, 2), 2)
    z = lax.div(md, 4)
    sibling = (st, md + 1 - 2 * core)
    across = (st, md + 2 - 4 * x)
    others = [(lax.rem(st + d, states), md) for d in range(1, states)]
    along = [(st, lax.rem(z + d, ring) * 4 + x * 2 + core) for d in range(1, ring)]
    partners = others + [sibling, across] + along

    barrier = pltpu.get_barrier_semaphore()
    for device in partners:
        pl.semaphore_signal(barrier, inc=1, device_id=device, device_id_type=MESH)

    numbers = iter(range(10000))

    def copy_to(device, source, target):
        at = next(numbers)
        return pltpu.make_async_remote_copy(
            src_ref=source, dst_ref=target, send_sem=send.at[at], recv_sem=recv.at[at],
            device_id=device, device_id_type=MESH,
        )

    def pack(value):
        return jnp.concatenate([value[:half], value[half:]], axis=1)

    lane = lax.broadcasted_iota(jnp.int32, (1, 2 * n), 1)

    def lanes(first, second):
        return jnp.where(lane < n, first, second)

    def load_state(s, g, value):
        high, low = split(value)
        rows = pl.ds(g * n, n)
        a3[s, rows, 0:n] = high
        a3[s, rows, n : 2 * n] = low
        a3[s, rows, 2 * n : 3 * n] = high
        for t in range(2):
            aa[s, t * n : (t + 1) * n, g * 2 * n + t * n : g * 2 * n + (t + 1) * n] = high
            aa[s, (2 + t) * n : (3 + t) * n, g * 2 * n + t * n : g * 2 * n + (t + 1) * n] = low

    def weights_three(value):
        high, low = split(value)
        return jnp.concatenate([high, high, low], axis=1)

    def store_x(high_ref, low_ref, product, q, weight):
        for k in range(2):
            rows = pl.ds(pl.multiple_of((2 * q + k) * n, n), n)
            for g in range(grid):
                block = product[g * n : (g + 1) * n, k * 2 * n : (k + 1) * 2 * n]
                block = block * lanes(weight(k, 0, g), weight(k, 1, g))
                high, low = split(block)
                high_ref[rows, g * 2 * n : (g + 1) * 2 * n] = high
                low_ref[rows, g * 2 * n : (g + 1) * 2 * n] = low

    def field(high_ref, low_ref, s, i):
        rows = pl.ds(pl.multiple_of(i * 2 * n, 2 * n), 2 * n)
        both = dot_rows(high_ref[rows, :], aa[s])
        return both[:, : 2 * n] + both[:, 2 * n :] + dot_rows(low_ref[rows, :], aa[s, 0 : 2 * n])

    def store_field(targets, block, i):
        turned = block.T
        for t in range(2):
            ref, start = targets[t]
            columns = pl.ds(pl.multiple_of(start + i * 2 * n, 2 * n), 2 * n)
            for m in range(modes):
                top = t * n + m * share
                ref[m % 2, m // 2 % 2, m // 4, :, columns] = turned[top : top + share]

    def act(left, high_ref, low_ref, gp):
        columns = pl.ds(pl.multiple_of(gp * 4 * n, 4 * n), 4 * n)
        both = dot(left[...], high_ref[:, columns])
        total = both[: 2 * n] + both[2 * n :] + dot(left[0 : 2 * n], low_ref[:, columns])
        return [
            total[0:n, k * 2 * n : k * 2 * n + n] + total[n : 2 * n, k * 2 * n + n : (k + 1) * 2 * n]
            for k in range(2)
        ]

    for g in range(grid):
        gath[st, g] = pack(a_ref[g])
    pl.semaphore_wait(barrier, len(partners))
    coeff_copies = [copy_to(device, gath.at[st], gath.at[st]) for device in others]
    for c in coeff_copies:
        c.start()

    aa[...] = jnp.zeros_like(aa)
    for g in range(grid):
        load_state(st, g, a_ref[g])

    def diag_group(q, carry):
        value = jnp.concatenate(
            [dh3[t * count + 2 * q + k] for k in range(2) for t in range(2)], axis=0
        )
        product = dot_rows(a3[st], weights_three(value))
        store_x(xh, xl, product, q, lambda k, t, g: dv1[t * count + 2 * q + k, g])
        return carry

    lax.fori_loop(0, count // 2, diag_group, 0)

    def diag_field(i, carry):
        store_field(((buf0, 0), (buf1, 0)), field(xh, xl, st, i), i)
        return carry

    lax.fori_loop(0, count // 2, diag_field, 0)

    def core_start(i):
        c = copy_to(sibling, bufs[i].at[1 - core], ras[i])
        c.start()
        return c

    def x_start(i, c):
        c.wait()
        sbs[i][...] = bufs[i][core] + ras[i][...]
        c = copy_to(across, sbs[i].at[1 - x], rbs[i])
        c.start()
        return c

    def z_start(i, c):
        c.wait()
        scs[i][...] = sbs[i][x] + rbs[i][...]
        copies = [
            copy_to(device, scs[i].at[lax.rem(z + d + 1, ring)], rcs[i].at[d])
            for d, device in enumerate(along)
        ]
        for c in copies:
            c.start()
        return copies

    def finish(i, copies):
        for c in copies:
            c.wait()
        total = scs[i][z]
        for d in range(ring - 1):
            total = total + rcs[i][d]
        return total

    flight = [core_start(0), core_start(1)]

    for t in range(2):
        for j in range(count):
            high, low = split(dh2[t * count + j])
            hh[t * n : (t + 1) * n, j * n : (j + 1) * n] = high
            hh[(2 + t) * n : (3 + t) * n, j * n : (j + 1) * n] = low
    flight = [x_start(i, flight[i]) for i in range(2)]

    def diag_act(gp, carry):
        first, second = act(hh, xh, xl, gp)
        action_ref[2 * gp] = first
        action_ref[2 * gp + 1] = second
        return carry

    lax.fori_loop(0, grid // 2, diag_act, 0)

    for c in coeff_copies:
        c.wait()
    for d in range(1, states):
        s = lax.rem(st + d, states)
        for g in range(grid):
            packed = gath[s, g]
            load_state(s, g, jnp.concatenate([packed[:, :n], packed[:, n:]], axis=0))

    def row_of(q, k, t):
        return (t * pcount + 2 * q + k) * states + st

    def pair_group(q, carry):
        rows = [row_of(q, k, t) for k in range(2) for t in range(2)]
        value = [ch3[pairs[row, 2]] for row in rows]
        product = None
        for s in range(states):
            masked = jnp.concatenate(
                [v * flag(pairs[row, 1] == s) for v, row in zip(value, rows)], axis=0
            )
            part = dot_rows(a3[s], weights_three(masked))
            product = part if product is None else product + part
        store_x(yh, yl, product, q, lambda k, t, g: cv1[pairs[row_of(q, k, t), 2], g])
        return carry

    lax.fori_loop(0, pcount // 2, pair_group, 0)
    flight = [z_start(i, flight[i]) for i in range(2)]

    def pair_field(i, carry):
        total = None
        for s in range(states):
            mask = [
                lanes(*[flag(pairs[row_of(i, k, t), 0] == s) for t in range(2)]) for k in range(2)
            ]
            block = field(yh, yl, s, i)
            block = jnp.concatenate([block[:n] * mask[0], block[n:] * mask[1]], axis=0)
            total = block if total is None else total + block
        store_field(((buf2, 0), (buf2, pcount * n)), total, i)
        return carry

    lax.fori_loop(0, pcount // 2, pair_field, 0)
    pair_flight = core_start(2)

    for t in range(2):
        for j in range(pcount):
            row = (t * pcount + j) * states + st
            high, low = split(ch2[pairs[row, 2]])
            for s in range(states):
                keep = flag(pairs[row, 0] == s).astype(BF16)
                hp[s, t * n : (t + 1) * n, j * n : (j + 1) * n] = high * keep
                hp[s, (2 + t) * n : (3 + t) * n, j * n : (j + 1) * n] = low * keep
    pair_flight = x_start(2, pair_flight)

    act_copies = []
    for d in list(range(1, states)) + [0]:
        s = lax.rem(st + d, states)

        def pair_act(gp, carry, s=s, d=d):
            for k, block in enumerate(act(hp.at[s], yh, yl, gp)):
                if d == 0:
                    action_ref[2 * gp + k] = action_ref[2 * gp + k] + block
                else:
                    psum[d - 1, 2 * gp + k] = pack(block)
            return carry

        lax.fori_loop(0, grid // 2, pair_act, 0)
        if d > 0:
            c = copy_to(others[d - 1], psum.at[d - 1], arecv.at[d - 1])
            c.start()
            act_copies.append(c)

    pair_flight = z_start(2, pair_flight)
    diag_ref[:, 0 : count * n] = finish(0, flight[0])
    diag_ref[:, count * n : 2 * count * n] = finish(1, flight[1])

    gfield[st] = finish(2, pair_flight)
    field_copies = [copy_to(device, gfield.at[st], gfield.at[st]) for device in others]
    for c in field_copies:
        c.start()
    for c in act_copies:
        c.wait()
    for d in range(states - 1):
        for g in range(grid):
            packed = arecv[d, g]
            action_ref[g] = action_ref[g] + jnp.concatenate([packed[:, :n], packed[:, n:]], axis=0)
    for c in field_copies:
        c.wait()
    for i in range(2 * pcount):
        for s in range(states):
            rows3[i * states + s] = gfield[s, :, i * n : (i + 1) * n]
    for i in range(slots.shape[0]):
        row = slots[i]
        value = rows3[jnp.maximum(row, 0)]
        pair_ref[:, i * n : (i + 1) * n] = jnp.where(row >= 0, value, 0.0)


def per_device(coeffs, diag_h2, diag_h3, diag_v1, coup_h2, coup_h3, coup_v1, pairs, n, modes, states):
    grid = coeffs.shape[1]
    terms = diag_h2.shape[1]
    npairs = pairs.shape[0]
    owned = npairs // states
    most_slots = min(3 * owned, npairs - 1)
    share = n // modes
    ring = modes // 4
    order = jnp.arange(npairs, dtype=jnp.int32)
    mine = pairs[:, 0] == lax.axis_index("state")
    rank = jnp.sum(jnp.where(mine[None, :] & (order[None, :] < order[:, None]), 1, 0), axis=1)
    hit = mine[None, :] & (rank[None, :] == jnp.arange(most_slots, dtype=jnp.int32)[:, None])
    slots = jnp.sum(jnp.where(hit, order[None, :] + 1, 0), axis=1).astype(jnp.int32) - 1

    widths = (terms // 2 * n, terms // 2 * n, owned * n)
    vmem = pltpu.VMEM
    scratch = [
        vmem((states, grid, n // 2, 2 * n), F32),
        vmem((states, grid * n, 3 * n), BF16),
        vmem((states, 4 * n, grid * 2 * n), BF16),
        vmem((4 * n, terms // 2 * n), BF16),
        vmem((states, 4 * n, owned // 2 * n), BF16),
        vmem((terms // 2 * n, grid * 2 * n), BF16),
        vmem((terms // 2 * n, grid * 2 * n), BF16),
        vmem((owned // 2 * n, grid * 2 * n), BF16),
        vmem((owned // 2 * n, grid * 2 * n), BF16),
        vmem((states - 1, grid, n // 2, 2 * n), F32),
        vmem((states - 1, grid, n // 2, 2 * n), F32),
        vmem((states, share, owned * n), F32),
        vmem((npairs, share, n), F32),
    ]
    for lead in ((2, 2, ring), (2, ring), (2, ring), (ring,), (ring,), (ring - 1,)):
        scratch += [vmem(lead + (share, w), F32) for w in widths]
    copies = 3 * (states - 1) + 3 * (ring + 1)
    scratch += [pltpu.SemaphoreType.DMA((copies,)), pltpu.SemaphoreType.DMA((copies,))]
    in_vmem = pl.BlockSpec(memory_space=pltpu.VMEM)
    in_smem = pl.BlockSpec(memory_space=pltpu.SMEM)
    action, diag, pair = pl.pallas_call(
        functools.partial(kernel, modes=modes),
        out_shape=(
            jax.ShapeDtypeStruct((grid, n, n), F32),
            jax.ShapeDtypeStruct((share, terms * n), F32),
            jax.ShapeDtypeStruct((share, most_slots * n), F32),
        ),
        in_specs=[in_vmem] * 5 + [in_smem] * 4,
        out_specs=(in_vmem,) * 3,
        scratch_shapes=scratch,
        compiler_params=pltpu.CompilerParams(
            collective_id=0, has_side_effects=True, vmem_limit_bytes=48 * 1024 * 1024
        ),
    )(
        coeffs.reshape(grid, n, n),
        diag_h2.reshape(terms, n, n),
        diag_h3.reshape(terms, n, n),
        coup_h2.reshape(-1, n, n),
        coup_h3.reshape(-1, n, n),
        diag_v1[0],
        coup_v1,
        pairs,
        slots,
    )
    return action.reshape(1, grid, n * n), diag[None], pair[None]


def solution(mesh):
    placed = (
        P("state", "mode", None),
        P("state", None, None),
        P("state", None, None),
        P("state", None, "mode"),
        P(),
        P(),
        P(None, "mode"),
        P(),
    )
    body = functools.partial(
        per_device, n=64, modes=mesh.shape["mode"], states=mesh.shape["state"]
    )
    return jax.shard_map(
        body,
        mesh=mesh,
        in_specs=placed,
        out_specs=(P("state", "mode", None),) * 3,
        check_vma=False,
    )
```

```python
import functools

import jax
import jax.numpy as jnp
from jax import lax
from jax.experimental import pallas as pl
from jax.experimental.pallas import tpu as pltpu
from jax.sharding import PartitionSpec as P

MESH = pl.DeviceIdType.MESH
F32 = jnp.float32
BF16 = jnp.bfloat16


def split(value):
    high = value.astype(BF16)
    return high, (value - high.astype(F32)).astype(BF16)


def dot_rows(left, right):
    return lax.dot_general(left, right, (((1,), (1,)), ((), ())), preferred_element_type=F32)


def dot(left, right):
    return jnp.dot(left, right, preferred_element_type=F32)


def flag(condition):
    return jnp.where(condition, 1.0, 0.0).astype(F32)


def kernel(
    a_ref, dh2, dh3, ch2, ch3, dv1, cv1, pairs, slots,
    action_ref, diag_ref, pair_ref,
    gath, d3, c2, c3, acc, a3, aa, hh, hp, xh, xl, yh, yl, psum, arecv, gfield, rows3,
    buf0, buf1, buf2, ra0, ra1, ra2, sb0, sb1, sb2, rb0, rb1, rb2, sc0, sc1, sc2, rc0, rc1, rc2,
    send, recv, *, modes
):
    states, grid = gath.shape[0], gath.shape[1]
    n = d3.shape[-1]
    half = n // 2
    count = dh2.shape[0] // 2
    pcount = yh.shape[0] // n
    ring = modes // 4
    share = n // modes
    bufs, ras, sbs = (buf0, buf1, buf2), (ra0, ra1, ra2), (sb0, sb1, sb2)
    rbs, scs, rcs = (rb0, rb1, rb2), (sc0, sc1, sc2), (rc0, rc1, rc2)

    st = lax.axis_index("state")
    md = lax.axis_index("mode")
    core = lax.rem(md, 2)
    x = lax.rem(lax.div(md, 2), 2)
    z = lax.div(md, 4)
    sibling = (st, md + 1 - 2 * core)
    across = (st, md + 2 - 4 * x)
    others = [(lax.rem(st + d, states), md) for d in range(1, states)]
    along = [(st, lax.rem(z + d, ring) * 4 + x * 2 + core) for d in range(1, ring)]
    partners = others + [sibling, across] + along

    barrier = pltpu.get_barrier_semaphore()
    for device in partners:
        pl.semaphore_signal(barrier, inc=1, device_id=device, device_id_type=MESH)

    numbers = iter(range(10000))

    def copy_to(device, source, target):
        at = next(numbers)
        return pltpu.make_async_remote_copy(
            src_ref=source, dst_ref=target, send_sem=send.at[at], recv_sem=recv.at[at],
            device_id=device, device_id_type=MESH,
        )

    def loop(total, body, step=4):
        step = step if total % step == 0 else 1

        def run(i, carry):
            for k in range(step):
                body(i * step + k)
            return carry

        lax.fori_loop(0, total // step, run, 0)

    def matrices(value):
        return value.reshape(value.shape[0], n, n)

    def spread(source, target):
        for t in range(0, source.shape[0], 8):
            target[t : t + 8] = matrices(source[t : t + 8, :])

    def pack(value):
        return jnp.concatenate([value[:half], value[half:]], axis=1)

    lane = lax.broadcasted_iota(jnp.int32, (1, 2 * n), 1)

    def lanes(first, second):
        return jnp.where(lane < n, first, second)

    def load_state(s, g, value):
        high, low = split(value)
        rows = pl.ds(g * n, n)
        a3[s, rows, 0:n] = high
        a3[s, rows, n : 2 * n] = low
        a3[s, rows, 2 * n : 3 * n] = high
        for t in range(2):
            aa[s, t * n : (t + 1) * n, g * 2 * n + t * n : g * 2 * n + (t + 1) * n] = high
            aa[s, (2 + t) * n : (3 + t) * n, g * 2 * n + t * n : g * 2 * n + (t + 1) * n] = low

    def weights_three(value):
        high, low = split(value)
        return jnp.concatenate([high, high, low], axis=1)

    def store_x(high_ref, low_ref, product, q, weight):
        for k in range(2):
            rows = pl.ds(pl.multiple_of((2 * q + k) * n, n), n)
            for g in range(grid):
                block = product[g * n : (g + 1) * n, k * 2 * n : (k + 1) * 2 * n]
                block = block * lanes(weight(k, 0, g), weight(k, 1, g))
                high, low = split(block)
                high_ref[rows, g * 2 * n : (g + 1) * 2 * n] = high
                low_ref[rows, g * 2 * n : (g + 1) * 2 * n] = low

    def field(high_ref, low_ref, s, i):
        rows = pl.ds(pl.multiple_of(i * 2 * n, 2 * n), 2 * n)
        both = dot_rows(high_ref[rows, :], aa[s])
        return both[:, : 2 * n] + both[:, 2 * n :] + dot_rows(low_ref[rows, :], aa[s, 0 : 2 * n])

    def store_field(targets, block, i):
        turned = block.T
        for t in range(2):
            ref, start = targets[t]
            columns = pl.ds(pl.multiple_of(start + i * 2 * n, 2 * n), 2 * n)
            for m in range(modes):
                top = t * n + m * share
                ref[m % 2, m // 2 % 2, m // 4, :, columns] = turned[top : top + share]

    def act(left, high_ref, low_ref, gp):
        columns = pl.ds(pl.multiple_of(gp * 4 * n, 4 * n), 4 * n)
        both = dot(left[...], high_ref[:, columns])
        total = both[: 2 * n] + both[2 * n :] + dot(left[0 : 2 * n], low_ref[:, columns])
        return [
            total[0:n, k * 2 * n : k * 2 * n + n] + total[n : 2 * n, k * 2 * n + n : (k + 1) * 2 * n]
            for k in range(2)
        ]

    aa[...] = jnp.zeros_like(aa)
    pl.semaphore_wait(barrier, len(partners))
    coeff_copies = [copy_to(device, a_ref, gath.at[st]) for device in others]
    for c in coeff_copies:
        c.start()

    tensor = matrices(a_ref[...])
    for g in range(grid):
        load_state(st, g, tensor[g])
    spread(dh3, d3)

    def diag_group(q):
        value = jnp.concatenate(
            [d3[t * count + 2 * q + k] for k in range(2) for t in range(2)], axis=0
        )
        product = dot_rows(a3[st], weights_three(value))
        store_x(xh, xl, product, q, lambda k, t, g: dv1[t * count + 2 * q + k, g])

    loop(count // 2, diag_group)

    def diag_field(i):
        store_field(((buf0, 0), (buf1, 0)), field(xh, xl, st, i), i)

    loop(count // 2, diag_field)

    def core_start(i):
        c = copy_to(sibling, bufs[i].at[1 - core], ras[i])
        c.start()
        return c

    def x_start(i, c):
        c.wait()
        sbs[i][...] = bufs[i][core] + ras[i][...]
        c = copy_to(across, sbs[i].at[1 - x], rbs[i])
        c.start()
        return c

    def z_start(i, c):
        c.wait()
        scs[i][...] = sbs[i][x] + rbs[i][...]
        copies = [
            copy_to(device, scs[i].at[lax.rem(z + d + 1, ring)], rcs[i].at[d])
            for d, device in enumerate(along)
        ]
        for c in copies:
            c.start()
        return copies

    def finish(i, copies):
        for c in copies:
            c.wait()
        total = scs[i][z]
        for d in range(ring - 1):
            total = total + rcs[i][d]
        return total

    flight = [core_start(0), core_start(1)]

    spread(ch3, c3)
    spread(ch2, c2)
    flight = [x_start(i, flight[i]) for i in range(2)]

    for c in coeff_copies:
        c.wait()
    for d in range(1, states):
        s = lax.rem(st + d, states)
        tensor = matrices(gath[s])
        for g in range(grid):
            load_state(s, g, tensor[g])

    def row_of(q, k, t):
        return (t * pcount + 2 * q + k) * states + st

    def pair_group(q):
        rows = [row_of(q, k, t) for k in range(2) for t in range(2)]
        value = [c3[pairs[row, 2]] for row in rows]
        product = None
        for s in range(states):
            masked = jnp.concatenate(
                [v * flag(pairs[row, 1] == s) for v, row in zip(value, rows)], axis=0
            )
            part = dot_rows(a3[s], weights_three(masked))
            product = part if product is None else product + part
        store_x(yh, yl, product, q, lambda k, t, g: cv1[pairs[row_of(q, k, t), 2], g])

    loop(pcount // 2, pair_group)
    flight = [z_start(i, flight[i]) for i in range(2)]

    def pair_field(i):
        total = None
        for s in range(states):
            mask = [
                lanes(*[flag(pairs[row_of(i, k, t), 0] == s) for t in range(2)]) for k in range(2)
            ]
            block = field(yh, yl, s, i)
            block = jnp.concatenate([block[:n] * mask[0], block[n:] * mask[1]], axis=0)
            total = block if total is None else total + block
        store_field(((buf2, 0), (buf2, pcount * n)), total, i)

    loop(pcount // 2, pair_field)
    pair_flight = core_start(2)

    for t in range(2):
        for j in range(pcount):
            row = (t * pcount + j) * states + st
            high, low = split(c2[pairs[row, 2]])
            for s in range(states):
                keep = flag(pairs[row, 0] == s).astype(BF16)
                hp[s, t * n : (t + 1) * n, j * n : (j + 1) * n] = high * keep
                hp[s, (2 + t) * n : (3 + t) * n, j * n : (j + 1) * n] = low * keep
    pair_flight = x_start(2, pair_flight)

    act_copies = []
    for d in list(range(1, states)) + [0]:
        s = lax.rem(st + d, states)

        def pair_act(gp, s=s, d=d):
            for k, block in enumerate(act(hp.at[s], yh, yl, gp)):
                if d == 0:
                    acc[2 * gp + k] = block
                else:
                    psum[d - 1, 2 * gp + k] = pack(block)

        loop(grid // 2, pair_act)
        if d > 0:
            c = copy_to(others[d - 1], psum.at[d - 1], arecv.at[d - 1])
            c.start()
            act_copies.append(c)
        if d == states - 1:
            pair_flight = z_start(2, pair_flight)

    for t in range(0, 2 * count, 8):
        value = matrices(dh2[t : t + 8, :])
        for k in range(8):
            top, j = (t + k) // count * n, (t + k) % count
            high, low = split(value[k])
            hh[top : top + n, j * n : (j + 1) * n] = high
            hh[2 * n + top : 3 * n + top, j * n : (j + 1) * n] = low

    def diag_act(gp):
        for k, block in enumerate(act(hh, xh, xl, gp)):
            acc[2 * gp + k] = acc[2 * gp + k] + block

    loop(grid // 2, diag_act, 2)
    gfield[st] = finish(2, pair_flight)
    field_copies = [copy_to(device, gfield.at[st], gfield.at[st]) for device in others]
    for c in field_copies:
        c.start()
    diag_ref[:, 0 : count * n] = finish(0, flight[0])
    diag_ref[:, count * n : 2 * count * n] = finish(1, flight[1])
    for c in act_copies:
        c.wait()
    for g in range(grid):
        total = acc[g]
        for d in range(states - 1):
            packed = arecv[d, g]
            total = total + jnp.concatenate([packed[:, :n], packed[:, n:]], axis=0)
        acc[g] = total
    action_ref[...] = jnp.concatenate(
        [acc[:, pl.ds(0, half, 2), :], acc[:, pl.ds(1, half, 2), :]], axis=-1
    ).reshape(grid, n * n)
    for c in field_copies:
        c.wait()
    for i in range(2 * pcount):
        for s in range(states):
            rows3[i * states + s] = gfield[s, :, i * n : (i + 1) * n]
    for i in range(slots.shape[0]):
        row = slots[i]
        value = rows3[jnp.maximum(row, 0)]
        pair_ref[:, i * n : (i + 1) * n] = jnp.where(row >= 0, value, 0.0)


def per_device(coeffs, diag_h2, diag_h3, diag_v1, coup_h2, coup_h3, coup_v1, pairs, n, modes, states):
    grid = coeffs.shape[1]
    terms = diag_h2.shape[1]
    npairs = pairs.shape[0]
    owned = npairs // states
    most_slots = min(3 * owned, npairs - 1)
    share = n // modes
    ring = modes // 4
    order = jnp.arange(npairs, dtype=jnp.int32)
    mine = pairs[:, 0] == lax.axis_index("state")
    rank = jnp.sum(jnp.where(mine[None, :] & (order[None, :] < order[:, None]), 1, 0), axis=1)
    hit = mine[None, :] & (rank[None, :] == jnp.arange(most_slots, dtype=jnp.int32)[:, None])
    slots = jnp.sum(jnp.where(hit, order[None, :] + 1, 0), axis=1).astype(jnp.int32) - 1

    widths = (terms // 2 * n, terms // 2 * n, owned * n)
    vmem = pltpu.VMEM
    scratch = [
        vmem((states, grid, n * n), F32),
        vmem((terms, n, n), F32),
        vmem(coup_h2.shape[:1] + (n, n), F32),
        vmem(coup_h2.shape[:1] + (n, n), F32),
        vmem((grid, n, n), F32),
        vmem((states, grid * n, 3 * n), BF16),
        vmem((states, 4 * n, grid * 2 * n), BF16),
        vmem((4 * n, terms // 2 * n), BF16),
        vmem((states, 4 * n, owned // 2 * n), BF16),
        vmem((terms // 2 * n, grid * 2 * n), BF16),
        vmem((terms // 2 * n, grid * 2 * n), BF16),
        vmem((owned // 2 * n, grid * 2 * n), BF16),
        vmem((owned // 2 * n, grid * 2 * n), BF16),
        vmem((states - 1, grid, n // 2, 2 * n), F32),
        vmem((states - 1, grid, n // 2, 2 * n), F32),
        vmem((states, share, owned * n), F32),
        vmem((npairs, share, n), F32),
    ]
    for lead in ((2, 2, ring), (2, ring), (2, ring), (ring,), (ring,), (ring - 1,)):
        scratch += [vmem(lead + (share, w), F32) for w in widths]
    copies = 3 * (states - 1) + 3 * (ring + 1)
    scratch += [pltpu.SemaphoreType.DMA((copies,)), pltpu.SemaphoreType.DMA((copies,))]
    in_vmem = pl.BlockSpec(memory_space=pltpu.VMEM)
    in_smem = pl.BlockSpec(memory_space=pltpu.SMEM)
    action, diag, pair = pl.pallas_call(
        functools.partial(kernel, modes=modes),
        out_shape=(
            jax.ShapeDtypeStruct((grid, n * n), F32),
            jax.ShapeDtypeStruct((share, terms * n), F32),
            jax.ShapeDtypeStruct((share, most_slots * n), F32),
        ),
        in_specs=[in_vmem] * 5 + [in_smem] * 4,
        out_specs=(in_vmem,) * 3,
        scratch_shapes=scratch,
        compiler_params=pltpu.CompilerParams(
            collective_id=0, has_side_effects=True, vmem_limit_bytes=48 * 1024 * 1024
        ),
    )(
        coeffs[0],
        diag_h2[0],
        diag_h3[0],
        coup_h2,
        coup_h3,
        diag_v1[0],
        coup_v1,
        pairs,
        slots,
    )
    return action[None], diag[None], pair[None]


def solution(mesh):
    placed = (
        P("state", "mode", None),
        P("state", None, None),
        P("state", None, None),
        P("state", None, "mode"),
        P(),
        P(),
        P(None, "mode"),
        P(),
    )
    body = functools.partial(
        per_device, n=64, modes=mesh.shape["mode"], states=mesh.shape["state"]
    )
    return jax.shard_map(
        body,
        mesh=mesh,
        in_specs=placed,
        out_specs=(P("state", "mode", None),) * 3,
        check_vma=False,
    )
```

```python
import functools

import jax
import jax.numpy as jnp
from jax import lax
from jax.experimental import pallas as pl
from jax.experimental.pallas import tpu as pltpu
from jax.sharding import PartitionSpec as P

MESH = pl.DeviceIdType.MESH
F32 = jnp.float32
BF16 = jnp.bfloat16


def split(value):
    high = value.astype(BF16)
    return high, (value - high.astype(F32)).astype(BF16)


def dot(left, right):
    return jnp.dot(left, right, preferred_element_type=F32)


def flag(condition):
    return jnp.where(condition, 1.0, 0.0).astype(F32)


def kernel(
    a_hbm, dh2_hbm, dh3_hbm, ch2_hbm, ch3_hbm, dv1, cv1, pairs, slots,
    action_ref, diag_ref, pair_ref,
    a_ref, dh2, dh3, ch2, ch3, gath, d3, c2, c3, acc, a3, aa, hh, hp, xh, xl, yh, yl, psum, arecv, gfield, rows3,
    buf0, buf1, buf2, ra0, ra1, ra2, sb0, sb1, sb2, rb0, rb1, rb2, sc0, sc1, sc2, rc0, rc1, rc2,
    send, recv, load, *, modes
):
    states, grid = gath.shape[0], gath.shape[1]
    n = d3.shape[-1]
    half = n // 2
    count = dh2.shape[0] // 2
    pcount = yh.shape[0] // n
    ring = modes // 4
    share = n // modes
    bufs, ras, sbs = (buf0, buf1, buf2), (ra0, ra1, ra2), (sb0, sb1, sb2)
    rbs, scs, rcs = (rb0, rb1, rb2), (sc0, sc1, sc2), (rc0, rc1, rc2)

    st = lax.axis_index("state")
    md = lax.axis_index("mode")
    core = lax.rem(md, 2)
    x = lax.rem(lax.div(md, 2), 2)
    z = lax.div(md, 4)
    sibling = (st, md + 1 - 2 * core)
    across = (st, md + 2 - 4 * x)
    others = [(lax.rem(st + d, states), md) for d in range(1, states)]
    along = [(st, lax.rem(z + d, ring) * 4 + x * 2 + core) for d in range(1, ring)]
    partners = others + [sibling, across] + along

    loads = [
        pltpu.make_async_copy(source, target, load.at[i])
        for i, (source, target) in enumerate(
            ((a_hbm, a_ref), (dh3_hbm, dh3), (ch3_hbm, ch3), (ch2_hbm, ch2), (dh2_hbm, dh2))
        )
    ]
    barrier = pltpu.get_barrier_semaphore()
    for device in partners:
        pl.semaphore_signal(barrier, inc=1, device_id=device, device_id_type=MESH)

    for c in loads:
        c.start()

    numbers = iter(range(10000))

    def copy_to(device, source, target):
        at = next(numbers)
        return pltpu.make_async_remote_copy(
            src_ref=source, dst_ref=target, send_sem=send.at[at], recv_sem=recv.at[at],
            device_id=device, device_id_type=MESH,
        )

    def loop(total, body, step=4):
        step = step if total % step == 0 else 1

        def run(i, carry):
            for k in range(step):
                body(i * step + k)
            return carry

        lax.fori_loop(0, total // step, run, 0)

    def matrices(value):
        return value.reshape(value.shape[0], n, n)

    def spread(source, target):
        for t in range(0, source.shape[0], 8):
            target[t : t + 8] = matrices(source[t : t + 8, :])

    def pack(value):
        return jnp.concatenate([value[:half], value[half:]], axis=1)

    lane = lax.broadcasted_iota(jnp.int32, (1, 2 * n), 1)

    def lanes(first, second):
        return jnp.where(lane < n, first, second)

    def load_state(s, g, value):
        high, low = split(value)
        rows = pl.ds(g * n, n)
        a3[s, rows, 0:n] = high
        a3[s, rows, n : 2 * n] = low
        a3[s, rows, 2 * n : 3 * n] = high
        high, low = split(value.T)
        for t in range(2):
            rows = pl.ds((2 * g + t) * n, n)
            aa[s, rows, t * n : (t + 1) * n] = high
            aa[s, rows, (2 + t) * n : (3 + t) * n] = low

    def weights_three(value):
        high, low = split(value)
        return jnp.concatenate([high, high, low], axis=0)

    def store_x(high_ref, low_ref, product, q, weight):
        for k in range(2):
            rows = pl.ds(pl.multiple_of((2 * q + k) * n, n), n)
            for g in range(grid):
                block = product[g * n : (g + 1) * n, k * 2 * n : (k + 1) * 2 * n]
                block = block * lanes(weight(k, 0, g), weight(k, 1, g))
                high, low = split(block)
                high_ref[rows, g * 2 * n : (g + 1) * 2 * n] = high
                low_ref[rows, g * 2 * n : (g + 1) * 2 * n] = low

    def field(high_ref, low_ref, s, rows):
        both = dot(high_ref[rows, :], aa[s])
        return both[:, : 2 * n] + both[:, 2 * n :] + dot(low_ref[rows, :], aa[s, :, 0 : 2 * n])

    def store_field(targets, block, i):
        turned = block.T
        for t in range(2):
            ref, start = targets[t]
            columns = pl.ds(pl.multiple_of(start + i * 2 * n, 2 * n), 2 * n)
            for m in range(modes):
                top = t * n + m * share
                ref[m % 2, m // 2 % 2, m // 4, :, columns] = turned[top : top + share]

    def act(left, high_ref, low_ref, gp):
        columns = pl.ds(pl.multiple_of(gp * 4 * n, 4 * n), 4 * n)
        size = left.shape[0] // 2
        both = dot(left[...], high_ref[:, columns])
        total = both[:size] + both[size:] + dot(left[0:size], low_ref[:, columns])
        return [
            [
                total[r : r + n, k * 2 * n : k * 2 * n + n]
                + total[r + n : r + 2 * n, k * 2 * n + n : (k + 1) * 2 * n]
                for k in range(2)
            ]
            for r in range(0, size, 2 * n)
        ]

    aa[...] = jnp.zeros_like(aa)
    loads[0].wait()
    pl.semaphore_wait(barrier, len(partners))
    coeff_copies = [copy_to(device, a_ref, gath.at[st]) for device in others]
    for c in coeff_copies:
        c.start()

    tensor = matrices(a_ref[...])
    for g in range(grid):
        load_state(st, g, tensor[g])
    loads[1].wait()
    spread(dh3, d3)

    def diag_group(q):
        value = jnp.concatenate(
            [d3[t * count + 2 * q + k] for k in range(2) for t in range(2)], axis=0
        )
        product = dot(a3[st], weights_three(value.T))
        store_x(xh, xl, product, q, lambda k, t, g: dv1[t * count + 2 * q + k, g])

    loop(count // 2, diag_group)

    part = min(count, 8)

    def diag_field(i):
        rows = pl.ds(pl.multiple_of(i * part * n, part * n), part * n)
        total = field(xh, xl, st, rows)
        for k in range(part // 2):
            block = total[k * 2 * n : (k + 1) * 2 * n]
            store_field(((buf0, 0), (buf1, 0)), block, i * (part // 2) + k)

    loop(count // part, diag_field, 1)

    def core_start(i):
        c = copy_to(sibling, bufs[i].at[1 - core], ras[i])
        c.start()
        return c

    def x_start(i, c):
        c.wait()
        sbs[i][...] = bufs[i][core] + ras[i][...]
        c = copy_to(across, sbs[i].at[1 - x], rbs[i])
        c.start()
        return c

    def z_start(i, c):
        c.wait()
        scs[i][...] = sbs[i][x] + rbs[i][...]
        copies = [
            copy_to(device, scs[i].at[lax.rem(z + d + 1, ring)], rcs[i].at[d])
            for d, device in enumerate(along)
        ]
        for c in copies:
            c.start()
        return copies

    def finish(i, copies):
        for c in copies:
            c.wait()
        total = scs[i][z]
        for d in range(ring - 1):
            total = total + rcs[i][d]
        return total

    flight = [core_start(0), core_start(1)]

    loads[2].wait()
    spread(ch3, c3)
    loads[3].wait()
    spread(ch2, c2)
    flight = [x_start(i, flight[i]) for i in range(2)]

    for c in coeff_copies:
        c.wait()
    for d in range(1, states):
        s = lax.rem(st + d, states)
        tensor = matrices(gath[s])
        for g in range(grid):
            load_state(s, g, tensor[g])

    def row_of(q, k, t):
        return (t * pcount + 2 * q + k) * states + st

    def pair_group(q):
        rows = [row_of(q, k, t) for k in range(2) for t in range(2)]
        value = [c3[pairs[row, 2]] for row in rows]
        value = jnp.concatenate(value, axis=0).T
        product = None
        for s in range(states):
            keep = [flag(pairs[row, 1] == s) for row in rows]
            keep = jnp.concatenate([lanes(keep[0], keep[1]), lanes(keep[2], keep[3])], axis=1)
            part = dot(a3[s], weights_three(value * keep))
            product = part if product is None else product + part
        store_x(yh, yl, product, q, lambda k, t, g: cv1[pairs[row_of(q, k, t), 2], g])

    loop(pcount // 2, pair_group)
    flight = [z_start(i, flight[i]) for i in range(2)]

    total = None
    for s in range(states):
        block = field(yh, yl, s, slice(None))
        keep = [
            lanes(*[flag(pairs[(t * pcount + j) * states + st, 0] == s) for t in range(2)])
            for j in range(pcount)
        ]
        block = jnp.concatenate(
            [block[j * n : (j + 1) * n] * keep[j] for j in range(pcount)], axis=0
        )
        total = block if total is None else total + block
    for i in range(pcount // 2):
        store_field(((buf2, 0), (buf2, pcount * n)), total[i * 2 * n : (i + 1) * 2 * n], i)
    pair_flight = core_start(2)

    for t in range(2):
        for j in range(pcount):
            row = (t * pcount + j) * states + st
            high, low = split(c2[pairs[row, 2]])
            for s in range(states):
                keep = flag(pairs[row, 0] == s).astype(BF16)
                top, low_top = (2 * s + t) * n, (2 * states + 2 * s + t) * n
                hp[top : top + n, j * n : (j + 1) * n] = high * keep
                hp[low_top : low_top + n, j * n : (j + 1) * n] = low * keep
    pair_flight = x_start(2, pair_flight)

    def pair_act(gp):
        for s, blocks in enumerate(act(hp, yh, yl, gp)):
            for k in range(2):
                psum[s, 2 * gp + k] = pack(blocks[k])

    loop(grid // 2, pair_act)
    act_copies = [
        copy_to(device, psum.at[lax.rem(st + d + 1, states)], arecv.at[d])
        for d, device in enumerate(others)
    ]
    for c in act_copies:
        c.start()
    pair_flight = z_start(2, pair_flight)

    loads[4].wait()
    for t in range(0, 2 * count, 8):
        value = matrices(dh2[t : t + 8, :])
        for k in range(8):
            top, j = (t + k) // count * n, (t + k) % count
            high, low = split(value[k])
            hh[top : top + n, j * n : (j + 1) * n] = high
            hh[2 * n + top : 3 * n + top, j * n : (j + 1) * n] = low

    def diag_act(gp):
        for k, block in enumerate(act(hh, xh, xl, gp)[0]):
            acc[2 * gp + k] = block

    loop(grid // 2, diag_act)
    gfield[st] = finish(2, pair_flight)
    field_copies = [copy_to(device, gfield.at[st], gfield.at[st]) for device in others]
    for c in field_copies:
        c.start()
    diag_ref[:, 0 : count * n] = finish(0, flight[0])
    diag_ref[:, count * n : 2 * count * n] = finish(1, flight[1])
    for c in act_copies:
        c.wait()
    for g in range(grid):
        packed = psum[st, g]
        for d in range(states - 1):
            packed = packed + arecv[d, g]
        acc[g] = acc[g] + jnp.concatenate([packed[:, :n], packed[:, n:]], axis=0)
    action_ref[...] = jnp.concatenate(
        [acc[:, pl.ds(0, half, 2), :], acc[:, pl.ds(1, half, 2), :]], axis=-1
    ).reshape(grid, n * n)
    for c in field_copies:
        c.wait()
    for i in range(2 * pcount):
        for s in range(states):
            rows3[i * states + s] = gfield[s, :, i * n : (i + 1) * n]
    for i in range(slots.shape[0]):
        row = slots[i]
        value = rows3[jnp.maximum(row, 0)]
        pair_ref[:, i * n : (i + 1) * n] = jnp.where(row >= 0, value, 0.0)


def per_device(coeffs, diag_h2, diag_h3, diag_v1, coup_h2, coup_h3, coup_v1, pairs, n, modes, states):
    grid = coeffs.shape[1]
    terms = diag_h2.shape[1]
    npairs = pairs.shape[0]
    owned = npairs // states
    most_slots = min(3 * owned, npairs - 1)
    share = n // modes
    ring = modes // 4
    order = jnp.arange(npairs, dtype=jnp.int32)
    mine = pairs[:, 0] == lax.axis_index("state")
    rank = jnp.sum(jnp.where(mine[None, :] & (order[None, :] < order[:, None]), 1, 0), axis=1)
    hit = mine[None, :] & (rank[None, :] == jnp.arange(most_slots, dtype=jnp.int32)[:, None])
    slots = jnp.sum(jnp.where(hit, order[None, :] + 1, 0), axis=1).astype(jnp.int32) - 1

    widths = (terms // 2 * n, terms // 2 * n, owned * n)
    vmem = pltpu.VMEM
    scratch = [vmem(coeffs.shape[1:], F32), vmem(diag_h2.shape[1:], F32), vmem(diag_h3.shape[1:], F32)]
    scratch += [vmem(coup_h2.shape, F32), vmem(coup_h3.shape, F32)]
    scratch += [
        vmem((states, grid, n * n), F32),
        vmem((terms, n, n), F32),
        vmem(coup_h2.shape[:1] + (n, n), F32),
        vmem(coup_h2.shape[:1] + (n, n), F32),
        vmem((grid, n, n), F32),
        vmem((states, grid * n, 3 * n), BF16),
        vmem((states, grid * 2 * n, 4 * n), BF16),
        vmem((4 * n, terms // 2 * n), BF16),
        vmem((states * 4 * n, owned // 2 * n), BF16),
        vmem((terms // 2 * n, grid * 2 * n), BF16),
        vmem((terms // 2 * n, grid * 2 * n), BF16),
        vmem((owned // 2 * n, grid * 2 * n), BF16),
        vmem((owned // 2 * n, grid * 2 * n), BF16),
        vmem((states, grid, n // 2, 2 * n), F32),
        vmem((states - 1, grid, n // 2, 2 * n), F32),
        vmem((states, share, owned * n), F32),
        vmem((npairs, share, n), F32),
    ]
    for lead in ((2, 2, ring), (2, ring), (2, ring), (ring,), (ring,), (ring - 1,)):
        scratch += [vmem(lead + (share, w), F32) for w in widths]
    copies = 3 * (states - 1) + 3 * (ring + 1)
    scratch += [pltpu.SemaphoreType.DMA((copies,)), pltpu.SemaphoreType.DMA((copies,))]
    scratch += [pltpu.SemaphoreType.DMA((5,))]
    in_hbm = pl.BlockSpec(memory_space=pltpu.HBM)
    in_vmem = pl.BlockSpec(memory_space=pltpu.VMEM)
    in_smem = pl.BlockSpec(memory_space=pltpu.SMEM)
    action, diag, pair = pl.pallas_call(
        functools.partial(kernel, modes=modes),
        out_shape=(
            jax.ShapeDtypeStruct((grid, n * n), F32),
            jax.ShapeDtypeStruct((share, terms * n), F32),
            jax.ShapeDtypeStruct((share, most_slots * n), F32),
        ),
        in_specs=[in_hbm] * 5 + [in_smem] * 4,
        out_specs=(in_vmem,) * 3,
        scratch_shapes=scratch,
        compiler_params=pltpu.CompilerParams(
            collective_id=0, has_side_effects=True, vmem_limit_bytes=48 * 1024 * 1024
        ),
    )(
        coeffs[0],
        diag_h2[0],
        diag_h3[0],
        coup_h2,
        coup_h3,
        diag_v1[0],
        coup_v1,
        pairs,
        slots,
    )
    return action[None], diag[None], pair[None]


def solution(mesh):
    placed = (
        P("state", "mode", None),
        P("state", None, None),
        P("state", None, None),
        P("state", None, "mode"),
        P(),
        P(),
        P(None, "mode"),
        P(),
    )
    body = functools.partial(
        per_device, n=64, modes=mesh.shape["mode"], states=mesh.shape["state"]
    )
    return jax.shard_map(
        body,
        mesh=mesh,
        in_specs=placed,
        out_specs=(P("state", "mode", None),) * 3,
        check_vma=False,
    )
```

```python
import functools

import jax
import jax.numpy as jnp
from jax import lax
from jax.experimental import pallas as pl
from jax.experimental.pallas import tpu as pltpu
from jax.sharding import PartitionSpec as P

MESH = pl.DeviceIdType.MESH
F32 = jnp.float32
BF16 = jnp.bfloat16


def split(value):
    high = value.astype(BF16)
    return high, (value - high.astype(F32)).astype(BF16)


def dot(left, right):
    return jnp.dot(left, right, preferred_element_type=F32)


def flag(condition):
    return jnp.where(condition, 1.0, 0.0).astype(F32)


def kernel(
    a_hbm, dh2_hbm, dh3_hbm, ch2_hbm, ch3_hbm, dv1, cv1, pairs, slots,
    action_ref, diag_ref, pair_ref,
    a_ref, dh2, dh3, ch2, ch3, gath, d3, c2, c3, acc, a3, aa, hh, hp, xh, xl, yh, yl, psum, arecv, gfield, rows3,
    buf0, buf1, buf2, ra0, ra1, ra2, sb0, sb1, sb2, rb0, rb1, rb2, sc0, sc1, sc2, rc0, rc1, rc2,
    send, recv, load, *, modes
):
    states, grid = gath.shape[0], gath.shape[1]
    n = d3.shape[-1]
    half = n // 2
    count = dh2.shape[0] // 2
    pcount = yh.shape[0] // n
    ring = modes // 4
    share = n // modes
    bufs, ras, sbs = (buf0, buf1, buf2), (ra0, ra1, ra2), (sb0, sb1, sb2)
    rbs, scs, rcs = (rb0, rb1, rb2), (sc0, sc1, sc2), (rc0, rc1, rc2)

    st = lax.axis_index("state")
    md = lax.axis_index("mode")
    core = lax.rem(md, 2)
    x = lax.rem(lax.div(md, 2), 2)
    z = lax.div(md, 4)
    sibling = (st, md + 1 - 2 * core)
    across = (st, md + 2 - 4 * x)
    others = [(lax.rem(st + d, states), md) for d in range(1, states)]
    along = [(st, lax.rem(z + d, ring) * 4 + x * 2 + core) for d in range(1, ring)]
    partners = others + [sibling, across] + along

    loads = [
        pltpu.make_async_copy(source, target, load.at[i])
        for i, (source, target) in enumerate(
            ((a_hbm, a_ref), (dh3_hbm, dh3), (ch3_hbm, ch3), (ch2_hbm, ch2), (dh2_hbm, dh2))
        )
    ]
    barrier = pltpu.get_barrier_semaphore()
    for device in partners:
        pl.semaphore_signal(barrier, inc=1, device_id=device, device_id_type=MESH)

    for c in loads:
        c.start()

    numbers = iter(range(10000))

    def copy_to(device, source, target):
        at = next(numbers)
        return pltpu.make_async_remote_copy(
            src_ref=source, dst_ref=target, send_sem=send.at[at], recv_sem=recv.at[at],
            device_id=device, device_id_type=MESH,
        )

    def loop(total, body, step=4):
        step = step if total % step == 0 else 1

        def run(i, carry):
            for k in range(step):
                body(i * step + k)
            return carry

        lax.fori_loop(0, total // step, run, 0)

    def matrices(value):
        return value.reshape(value.shape[0], n, n)

    def spread(source, target):
        for t in range(0, source.shape[0], 8):
            target[t : t + 8] = matrices(source[t : t + 8, :])

    def pack(value):
        return jnp.concatenate([value[:half], value[half:]], axis=1)

    lane = lax.broadcasted_iota(jnp.int32, (1, 2 * n), 1)

    def lanes(first, second):
        return jnp.where(lane < n, first, second)

    def load_state(s, g, value):
        high, low = split(value)
        rows = pl.ds(g * n, n)
        a3[s, rows, 0:n] = high
        a3[s, rows, n : 2 * n] = low
        a3[s, rows, 2 * n : 3 * n] = high
        high, low = split(value.T)
        for t in range(2):
            rows = pl.ds((2 * g + t) * n, n)
            aa[s, rows, t * n : (t + 1) * n] = high
            aa[s, rows, (2 + t) * n : (3 + t) * n] = low

    def weights_three(value):
        high, low = split(value)
        return jnp.concatenate([high, high, low], axis=0)

    def store_x(high_ref, low_ref, product, q, weight):
        for k in range(2):
            rows = pl.ds(pl.multiple_of((2 * q + k) * n, n), n)
            for g in range(grid):
                block = product[g * n : (g + 1) * n, k * 2 * n : (k + 1) * 2 * n]
                block = block * lanes(weight(k, 0, g), weight(k, 1, g))
                high, low = split(block)
                high_ref[rows, g * 2 * n : (g + 1) * 2 * n] = high
                low_ref[rows, g * 2 * n : (g + 1) * 2 * n] = low

    def field(high_ref, low_ref, s, rows):
        both = dot(high_ref[rows, :], aa[s])
        return both[:, : 2 * n] + both[:, 2 * n :] + dot(low_ref[rows, :], aa[s, :, 0 : 2 * n])

    def store_field(targets, block, i):
        turned = block.T
        for t in range(2):
            ref, start = targets[t]
            columns = pl.ds(pl.multiple_of(start + i * 2 * n, 2 * n), 2 * n)
            for m in range(modes):
                top = t * n + m * share
                ref[m % 2, m // 2 % 2, m // 4, :, columns] = turned[top : top + share]

    def act(left, high_ref, low_ref, gp):
        columns = pl.ds(pl.multiple_of(gp * 4 * n, 4 * n), 4 * n)
        size = left.shape[0] // 2
        both = dot(left[...], high_ref[:, columns])
        total = both[:size] + both[size:] + dot(left[0:size], low_ref[:, columns])
        return [
            [
                total[r : r + n, k * 2 * n : k * 2 * n + n]
                + total[r + n : r + 2 * n, k * 2 * n + n : (k + 1) * 2 * n]
                for k in range(2)
            ]
            for r in range(0, size, 2 * n)
        ]

    aa[...] = jnp.zeros_like(aa)
    loads[0].wait()
    pl.semaphore_wait(barrier, len(partners))
    coeff_copies = [copy_to(device, a_ref, gath.at[st]) for device in others]
    for c in coeff_copies:
        c.start()

    tensor = matrices(a_ref[...])
    for g in range(grid):
        load_state(st, g, tensor[g])
    loads[1].wait()
    spread(dh3, d3)

    def diag_group(q):
        value = jnp.concatenate(
            [d3[t * count + 2 * q + k] for k in range(2) for t in range(2)], axis=0
        )
        product = dot(a3[st], weights_three(value.T))
        store_x(xh, xl, product, q, lambda k, t, g: dv1[t * count + 2 * q + k, g])

    loop(count // 2, diag_group)

    part = min(count, 8)

    def diag_field(i):
        rows = pl.ds(pl.multiple_of(i * part * n, part * n), part * n)
        total = field(xh, xl, st, rows)
        for k in range(part // 2):
            block = total[k * 2 * n : (k + 1) * 2 * n]
            store_field(((buf0, 0), (buf1, 0)), block, i * (part // 2) + k)

    loop(count // part, diag_field, 1)

    def core_start(i):
        c = copy_to(sibling, bufs[i].at[1 - core], ras[i])
        c.start()
        return c

    def x_start(i, c):
        c.wait()
        sbs[i][...] = bufs[i][core] + ras[i][...]
        c = copy_to(across, sbs[i].at[1 - x], rbs[i])
        c.start()
        return c

    def z_start(i, c):
        c.wait()
        scs[i][...] = sbs[i][x] + rbs[i][...]
        copies = [
            copy_to(device, scs[i].at[lax.rem(z + d + 1, ring)], rcs[i].at[d])
            for d, device in enumerate(along)
        ]
        for c in copies:
            c.start()
        return copies

    def finish(i, copies):
        for c in copies:
            c.wait()
        total = scs[i][z]
        for d in range(ring - 1):
            total = total + rcs[i][d]
        return total

    flight = [core_start(0), core_start(1)]

    loads[2].wait()
    spread(ch3, c3)
    loads[3].wait()
    spread(ch2, c2)
    flight = [x_start(i, flight[i]) for i in range(2)]

    for c in coeff_copies:
        c.wait()
    for d in range(1, states):
        s = lax.rem(st + d, states)
        tensor = matrices(gath[s])
        for g in range(grid):
            load_state(s, g, tensor[g])

    def row_of(q, k, t):
        return (t * pcount + 2 * q + k) * states + st

    def pair_group(q):
        rows = [row_of(q, k, t) for k in range(2) for t in range(2)]
        value = [c3[pairs[row, 2]] for row in rows]
        value = jnp.concatenate(value, axis=0).T
        product = None
        for s in range(states):
            keep = [flag(pairs[row, 1] == s) for row in rows]
            keep = jnp.concatenate([lanes(keep[0], keep[1]), lanes(keep[2], keep[3])], axis=1)
            part = dot(a3[s], weights_three(value * keep))
            product = part if product is None else product + part
        store_x(yh, yl, product, q, lambda k, t, g: cv1[pairs[row_of(q, k, t), 2], g])

    loop(pcount // 2, pair_group)
    flight = [z_start(i, flight[i]) for i in range(2)]

    total = None
    for s in range(states):
        block = field(yh, yl, s, slice(None))
        keep = [
            lanes(*[flag(pairs[(t * pcount + j) * states + st, 0] == s) for t in range(2)])
            for j in range(pcount)
        ]
        block = jnp.concatenate(
            [block[j * n : (j + 1) * n] * keep[j] for j in range(pcount)], axis=0
        )
        total = block if total is None else total + block
    for i in range(pcount // 2):
        store_field(((buf2, 0), (buf2, pcount * n)), total[i * 2 * n : (i + 1) * 2 * n], i)
    pair_flight = core_start(2)

    for t in range(2):
        for j in range(pcount):
            row = (t * pcount + j) * states + st
            high, low = split(c2[pairs[row, 2]])
            for s in range(states):
                keep = flag(pairs[row, 0] == s).astype(BF16)
                top, low_top = (2 * s + t) * n, (2 * states + 2 * s + t) * n
                hp[top : top + n, j * n : (j + 1) * n] = high * keep
                hp[low_top : low_top + n, j * n : (j + 1) * n] = low * keep
    pair_flight = x_start(2, pair_flight)

    def pair_act(gp):
        for s, blocks in enumerate(act(hp, yh, yl, gp)):
            for k in range(2):
                psum[s, 2 * gp + k] = pack(blocks[k])

    loop(grid // 2, pair_act)
    act_copies = [
        copy_to(device, psum.at[lax.rem(st + d + 1, states)], arecv.at[d])
        for d, device in enumerate(others)
    ]
    for c in act_copies:
        c.start()
    pair_flight = z_start(2, pair_flight)

    loads[4].wait()
    for t in range(0, 2 * count, 8):
        value = matrices(dh2[t : t + 8, :])
        for k in range(8):
            top, j = (t + k) // count * n, (t + k) % count
            high, low = split(value[k])
            hh[top : top + n, j * n : (j + 1) * n] = high
            hh[2 * n + top : 3 * n + top, j * n : (j + 1) * n] = low

    def diag_act(gp):
        for k, block in enumerate(act(hh, xh, xl, gp)[0]):
            acc[2 * gp + k] = block

    loop(grid // 2, diag_act)
    gfield[st] = finish(2, pair_flight)
    field_copies = [copy_to(device, gfield.at[st], gfield.at[st]) for device in others]
    for c in field_copies:
        c.start()
    diag_ref[:, 0 : count * n] = finish(0, flight[0])
    diag_ref[:, count * n : 2 * count * n] = finish(1, flight[1])
    for c in act_copies:
        c.wait()
    for g in range(grid):
        packed = psum[st, g]
        for d in range(states - 1):
            packed = packed + arecv[d, g]
        acc[g] = acc[g] + jnp.concatenate([packed[:, :n], packed[:, n:]], axis=0)
    action_ref[...] = jnp.concatenate(
        [acc[:, pl.ds(0, half, 2), :], acc[:, pl.ds(1, half, 2), :]], axis=-1
    ).reshape(grid, n * n)
    for c in field_copies:
        c.wait()
    for i in range(2 * pcount):
        for s in range(states):
            rows3[i * states + s] = gfield[s, :, i * n : (i + 1) * n]
    for i in range(slots.shape[0]):
        row = slots[i]
        value = rows3[jnp.maximum(row, 0)]
        pair_ref[:, i * n : (i + 1) * n] = jnp.where(row >= 0, value, 0.0)


def per_device(coeffs, diag_h2, diag_h3, diag_v1, coup_h2, coup_h3, coup_v1, pairs, n, modes, states):
    grid = coeffs.shape[1]
    terms = diag_h2.shape[1]
    npairs = pairs.shape[0]
    owned = npairs // states
    most_slots = min(3 * owned, npairs - 1)
    share = n // modes
    ring = modes // 4
    order = jnp.arange(npairs, dtype=jnp.int32)
    mine = pairs[:, 0] == lax.axis_index("state")
    rank = jnp.sum(jnp.where(mine[None, :] & (order[None, :] < order[:, None]), 1, 0), axis=1)
    hit = mine[None, :] & (rank[None, :] == jnp.arange(most_slots, dtype=jnp.int32)[:, None])
    slots = jnp.sum(jnp.where(hit, order[None, :] + 1, 0), axis=1).astype(jnp.int32) - 1

    widths = (terms // 2 * n, terms // 2 * n, owned * n)
    vmem = pltpu.VMEM
    scratch = [vmem(coeffs.shape[1:], F32), vmem(diag_h2.shape[1:], F32), vmem(diag_h3.shape[1:], F32)]
    scratch += [vmem(coup_h2.shape, F32), vmem(coup_h3.shape, F32)]
    scratch += [
        vmem((states, grid, n * n), F32),
        vmem((terms, n, n), F32),
        vmem(coup_h2.shape[:1] + (n, n), F32),
        vmem(coup_h2.shape[:1] + (n, n), F32),
        vmem((grid, n, n), F32),
        vmem((states, grid * n, 3 * n), BF16),
        vmem((states, grid * 2 * n, 4 * n), BF16),
        vmem((4 * n, terms // 2 * n), BF16),
        vmem((states * 4 * n, owned // 2 * n), BF16),
        vmem((terms // 2 * n, grid * 2 * n), BF16),
        vmem((terms // 2 * n, grid * 2 * n), BF16),
        vmem((owned // 2 * n, grid * 2 * n), BF16),
        vmem((owned // 2 * n, grid * 2 * n), BF16),
        vmem((states, grid, n // 2, 2 * n), F32),
        vmem((states - 1, grid, n // 2, 2 * n), F32),
        vmem((states, share, owned * n), F32),
        vmem((npairs, share, n), F32),
    ]
    for lead in ((2, 2, ring), (2, ring), (2, ring), (ring,), (ring,), (ring - 1,)):
        scratch += [vmem(lead + (share, w), F32) for w in widths]
    copies = 3 * (states - 1) + 3 * (ring + 1)
    scratch += [pltpu.SemaphoreType.DMA((copies,)), pltpu.SemaphoreType.DMA((copies,))]
    scratch += [pltpu.SemaphoreType.DMA((5,))]
    in_hbm = pl.BlockSpec(memory_space=pltpu.HBM)
    in_vmem = pl.BlockSpec(memory_space=pltpu.VMEM)
    in_smem = pl.BlockSpec(memory_space=pltpu.SMEM)
    action, diag, pair = pl.pallas_call(
        functools.partial(kernel, modes=modes),
        out_shape=(
            jax.ShapeDtypeStruct((grid, n * n), F32),
            jax.ShapeDtypeStruct((share, terms * n), F32),
            jax.ShapeDtypeStruct((share, most_slots * n), F32),
        ),
        in_specs=[in_hbm] * 5 + [in_smem] * 4,
        out_specs=(in_vmem,) * 3,
        scratch_shapes=scratch,
        compiler_params=pltpu.CompilerParams(
            collective_id=0, has_side_effects=True, vmem_limit_bytes=61 * 1024 * 1024
        ),
    )(
        coeffs[0],
        diag_h2[0],
        diag_h3[0],
        coup_h2,
        coup_h3,
        diag_v1[0],
        coup_v1,
        pairs,
        slots,
    )
    return action[None], diag[None], pair[None]


def solution(mesh):
    placed = (
        P("state", "mode", None),
        P("state", None, None),
        P("state", None, None),
        P("state", None, "mode"),
        P(),
        P(),
        P(None, "mode"),
        P(),
    )
    body = functools.partial(
        per_device, n=64, modes=mesh.shape["mode"], states=mesh.shape["state"]
    )
    return jax.shard_map(
        body,
        mesh=mesh,
        in_specs=placed,
        out_specs=(P("state", "mode", None),) * 3,
        check_vma=False,
    )
```
